256 devices in a mesh: seq: 128 (over z, x, y), head: 2 (over core).
Axes of the slice: x: 4, y: 4, z: 8, core: 2. Of those that a mesh axis runs over, the one named last changes fastest.
Arguments:
- queries: bfloat16 [32768, 4096], P('seq', 'head'), may hold values from -300 to 300
- keys: bfloat16 [32768, 512], P('seq', 'head'), may hold values from -8 to 8
- values: bfloat16 [32768, 512], P('seq', 'head'), may hold values from -24 to 24
- kept_count: int32 [128, 4], P('seq', 'head'), may hold values from 0 to 128, as said below
- kept_rows: int32 [128, 4, 128], P('seq', 'head'), may hold values from 0 to 255, as said below
Outputs:
- attended: bfloat16 [32768, 4096], P('seq', 'head')
The draws below stay inside these ranges and needn't reach their ends.
Inputs may be any that keep to these rules, and one draw needn't show every extreme that they name: `kept_count`: for each block and each index of head, exactly one of its 2 KV heads has 128 retained rows and the others have none. `kept_rows`: for each block and KV head, distinct rows in increasing order.
All inputs are finite; a program needn't handle non-finite values.
Results may differ from the reference program's by a relative error of at most 0.0055.
Values may be sent and summed in bfloat16 or wider, within the bound.
A program may use at most 64 MiB of HBM per device.

```python
import jax
import jax.numpy as jnp
from jax import lax

HD = 128
GROUP = 8
KV_DEV = 2
TOK_DEV = 256
PASS = 128
ANCHOR = 128
KVH = 4
HQ = 32
TOKENS = 32768
N_SEQ = 128


def shared_keys(key):
    base = jnp.clip(jax.random.normal(key, (TOKENS, KVH * HD), jnp.float32), -7.5, 7.5)
    token_ids = jnp.arange(TOKENS)
    following = jnp.roll(base, -1, axis=0)
    marked = ((token_ids + 1) % 53 == 0)[:, None]
    return jnp.where(marked, following, base)


def draw_keys(key, part):
    shared = shared_keys(key)
    return shared.astype(jnp.bfloat16)


def draw_queries(key, part):
    key = jax.random.fold_in(key, 7)
    fresh = jnp.clip(2.0 * jax.random.normal(key, (TOKENS, HQ * HD), jnp.float32), -12.0, 12.0)
    return fresh.astype(jnp.bfloat16)


def draw_kept_count(key, part):
    key = jax.random.fold_in(key, 3)
    owner = jax.random.randint(key, (N_SEQ, KVH // KV_DEV), 0, KV_DEV)
    local_ids = jnp.arange(KV_DEV, dtype=jnp.int32)
    table = (owner[:, :, None] == local_ids[None, None, :]).astype(jnp.int32) * PASS
    return table.reshape(N_SEQ, KVH)


def draw_kept_rows(key, part):
    key = jax.random.fold_in(key, 5)
    row_keys = jax.random.split(key, N_SEQ * KVH)
    chosen = jax.vmap(lambda sub_key: jax.random.permutation(sub_key, TOK_DEV)[:PASS])(row_keys)
    return jnp.sort(chosen, axis=-1).astype(jnp.int32).reshape(N_SEQ, KVH, PASS)


def shard_levels(rng, extent, pieces, low, largest):
    def one(dim, blocks):
        heights = jax.random.uniform(jax.random.fold_in(jax.random.fold_in(rng, 6), dim), (blocks,), jnp.float32, low / len(pieces), largest / len(pieces))
        return jnp.repeat(jnp.exp(heights), extent[dim] // blocks).reshape((-1,) + (1,) * (len(extent) - dim - 1))

    loudness = one(*pieces[0])
    for cut in pieces[1:]:
        loudness = loudness * one(*cut)
    return loudness


def noise(rng, dims, spread, most, cuts=(), kind=jnp.bfloat16):
    entries = spread * jax.random.normal(rng, dims, jnp.float32)
    if cuts:
        entries = entries * shard_levels(rng, dims, cuts, -0.22, 0.18)
    return jnp.clip(entries, -most, most).astype(kind)


def setup_inputs(seed: int = 0) -> dict:
    splits = jax.random.split(jax.random.key(seed), 6)
    queries = draw_queries(jax.random.fold_in(splits[5], 71), 0)
    keys = draw_keys(jax.random.fold_in(splits[5], 71), 0)
    values = noise(splits[2], (TOKENS, KVH * HD), 4.0, 24.0, ((0, 128), (1, 2)))
    kept_count = draw_kept_count(jax.random.fold_in(splits[5], 71), 0)
    kept_rows = draw_kept_rows(jax.random.fold_in(splits[5], 71), 0)
    return {"queries": queries, "keys": keys, "values": values, "kept_count": kept_count, "kept_rows": kept_rows}


masked_score = -1.0e30


def reference(queries, keys, values, kept_count, kept_rows):
    query_all = queries.reshape(N_SEQ, TOK_DEV, KVH, GROUP, HD)
    key_all = keys.reshape(N_SEQ, TOK_DEV, KVH, HD)
    value_all = values.reshape(N_SEQ, TOK_DEV, KVH, HD)
    picks = kept_rows.astype(jnp.int32)
    key_trans = jnp.transpose(key_all, (0, 2, 1, 3))
    value_trans = jnp.transpose(value_all, (0, 2, 1, 3))
    pass_keys = jnp.take_along_axis(key_trans, picks[..., None], axis=2)
    pass_values = jnp.take_along_axis(value_trans, picks[..., None], axis=2)
    slot_ids = jnp.arange(PASS, dtype=jnp.int32)
    slot_live = slot_ids[None, None, :] < kept_count.astype(jnp.int32)[:, :, None]
    pass_keys = jnp.transpose(pass_keys, (1, 0, 2, 3)).reshape(KVH, N_SEQ * PASS, HD)
    pass_values = jnp.transpose(pass_values, (1, 0, 2, 3)).reshape(KVH, N_SEQ * PASS, HD)
    slot_live = jnp.transpose(slot_live, (1, 0, 2)).reshape(KVH, N_SEQ * PASS)
    slot_host = jnp.repeat(jnp.arange(N_SEQ, dtype=jnp.int32), PASS)
    anchor_keys = jnp.transpose(key_all[0, :ANCHOR], (1, 0, 2))
    anchor_values = jnp.transpose(value_all[0, :ANCHOR], (1, 0, 2))
    token_ids = jnp.arange(TOK_DEV, dtype=jnp.int32)
    causal = token_ids[:, None] >= token_ids[None, :]
    score_scale = 1.0 / (HD ** 0.5)

    def host_attention(host_id):
        host_queries = jnp.transpose(query_all[host_id], (1, 2, 0, 3)).astype(jnp.float32)
        host_keys = jnp.transpose(key_all[host_id], (1, 0, 2))
        host_values = jnp.transpose(value_all[host_id], (1, 0, 2))
        seen_keys = jnp.concatenate([anchor_keys, pass_keys, host_keys], axis=1).astype(jnp.float32)
        seen_values = jnp.concatenate([anchor_values, pass_values, host_values], axis=1)
        live_anchor = jnp.broadcast_to(host_id >= 1, (KVH, TOK_DEV, ANCHOR))
        live_pass = jnp.broadcast_to((slot_live & (slot_host[None, :] < host_id))[:, None, :], (KVH, TOK_DEV, N_SEQ * PASS))
        live_local = jnp.broadcast_to(causal[None], (KVH, TOK_DEV, TOK_DEV))
        visible = jnp.concatenate([live_anchor, live_pass, live_local], axis=2)
        scores = jnp.einsum("gjtd,gsd->gjts", host_queries, seen_keys, precision=lax.Precision.HIGHEST) * score_scale
        scores = jnp.where(visible[:, None], scores, masked_score)
        top = jnp.max(scores, axis=-1, keepdims=True)
        raw_weights = jnp.exp(scores - top)
        totals = jnp.sum(raw_weights, axis=-1)
        weights = raw_weights.astype(jnp.bfloat16)
        mixed = jnp.einsum("gjts,gsd->gjtd", weights, seen_values, preferred_element_type=jnp.float32)
        mixed = mixed / totals[..., None]
        return jnp.transpose(mixed, (2, 0, 1, 3)).reshape(TOK_DEV, HQ * HD).astype(jnp.bfloat16)

    result = lax.map(host_attention, jnp.arange(N_SEQ, dtype=jnp.int32))
    return result.reshape(TOKENS, HQ * HD)
```

```python
import functools
import math

import jax
import jax.numpy as jnp
from jax import lax
from jax.experimental import pallas as pl
from jax.experimental.pallas import tpu as pltpu
from jax.sharding import PartitionSpec as P

F32 = jnp.float32
BF16 = jnp.bfloat16
HD = 128
TOK = 256
NZ, NX, NY = 8, 4, 4
PLANE = NX * NY
BLK = 272
CB = 8
NK = CB * 128
R = 1024
NR = 2
LOW = -1.0e30
HIGH = 1.0e30
CSC = math.log2(math.e) / math.sqrt(HD)


def dot(a, b):
    return jnp.dot(a, b, preferred_element_type=F32)


def dot_tn(a, b):
    return lax.dot_general(a, b, (((0,), (0,)), ((), ())), preferred_element_type=F32)


def widen(row):
    return jnp.concatenate([row] * (R // 128), axis=1)


def kernel(
    q_ref, k_ref, v_ref, cnt_ref, rows_ref, o_ref,
    kv, anc, qt, acc, mst, kc, vc, sb, pb, mb, shrink,
    rs, ss, zs, ars, ass,
):
    me = lax.axis_index("seq")
    z = me // PLANE
    x = (me % PLANE) // NY
    y = me % NY
    npairs = z // 2 + 1

    def seq_of(zz, xx, yy):
        return zz * PLANE + xx * NY + yy

    xp, xm, x2 = (x + 1) % NX, (x + NX - 1) % NX, (x + 2) % NX
    yp, ym, y2 = (y + 1) % NY, (y + NY - 1) % NY, (y + 2) % NY
    plus = {0: seq_of(z, x, yp), 1: seq_of(z, xp, y)}
    minus = {0: seq_of(z, x, ym), 1: seq_of(z, xm, y)}

    def remote(src, dst, send_sem, recv_sem, target):
        return pltpu.make_async_remote_copy(
            src_ref=src, dst_ref=dst, send_sem=send_sem, recv_sem=recv_sem,
            device_id={"seq": target}, device_id_type=pl.DeviceIdType.MESH,
        )

    barrier = pltpu.get_barrier_semaphore()
    for other in (plus[0], minus[0], plus[1], minus[1]):
        pl.semaphore_signal(barrier, inc=1, device_id={"seq": other}, device_id_type=pl.DeviceIdType.MESH)
    for dz in range(1, NZ):
        pl.semaphore_signal(
            barrier, inc=1, device_id={"seq": seq_of((z + dz) % NZ, x, y)}, device_id_type=pl.DeviceIdType.MESH
        )

    ksel = jnp.zeros((128, HD), F32)
    vsel = jnp.zeros((HD, 128), F32)
    tok_row = lax.broadcasted_iota(jnp.int32, (TOK, 128), 0)
    slot = lax.broadcasted_iota(jnp.int32, (1, 128), 1)
    for g in range(2):
        picks = jnp.where(slot < cnt_ref[0:1, g : g + 1], rows_ref[0, g : g + 1, :], -1)
        hot = jnp.where(tok_row == picks, 1.0, 0.0).astype(BF16)
        ksel = ksel + dot_tn(hot, k_ref[:, g * HD : (g + 1) * HD])
        vsel = vsel + dot_tn(v_ref[:, g * HD : (g + 1) * HD], hot)
    kv[z, x, y, 0:128, :] = ksel.astype(BF16)
    kv[z, x, y, 128:256, :] = vsel.astype(BF16)
    tag = jnp.where(cnt_ref[0:1, 1:2] > 0, 1.0, 0.0)
    kv[z, x, y, 256:272, :] = jnp.broadcast_to(tag, (16, 128)).astype(BF16)

    @pl.when(me == 0)
    def _():
        for g in range(2):
            anc[g, 0:128, :] = k_ref[0:128, g * HD : (g + 1) * HD]
            anc[g, 128:256, :] = v_ref[0:128, g * HD : (g + 1) * HD].T

    pl.semaphore_wait(barrier, 4 + NZ - 1)

    def lines(layer, role, at):
        return kv.at[layer, at] if role == 0 else kv.at[layer, :, at]

    def half(ref, which):
        n = len(ref.shape) - 2
        return ref.at[(slice(None),) * n + ((slice(0, 128) if which == 0 else slice(128, BLK)),)]

    own_at = {0: x, 1: y}
    minus_at = {0: xm, 1: ym}
    plus_at = {0: xp, 1: yp}
    far_at = {0: x2, 1: y2}

    def block(layer, role, at):
        return kv.at[layer, x, at] if role == 0 else kv.at[layer, at, y]

    b_own, b_minus, b_plus, b_far = {0: y, 1: x}, {0: ym, 1: xm}, {0: yp, 1: xp}, {0: y2, 1: x2}

    def zcopy(src_layer, target):
        ref = kv.at[src_layer, x, y]
        return remote(ref, ref, zs.at[target // PLANE], rs.at[src_layer, 0], target)

    def s1(layer, role, step):
        p, m = plus[role], minus[role]
        if step == 0:
            ref, target = block(layer, role, b_own[role]), p
        elif step == 1:
            ref, target = block(layer, role, b_own[role]), m
        elif step == 2:
            ref, target = half(block(layer, role, b_minus[role]), 0), p
        else:
            ref, target = half(block(layer, role, b_plus[role]), 1), m
        return remote(ref, ref, ss.at[layer, step], rs.at[layer, 1 + step], target)

    def s1_in(layer, role, step):
        if step == 0:
            ref = block(layer, role, b_minus[role])
        elif step == 1:
            ref = block(layer, role, b_plus[role])
        else:
            ref = half(block(layer, role, b_far[role]), step - 2)
        return remote(ref, ref, ss.at[layer, step], rs.at[layer, 1 + step], plus[role])

    def s2(layer, role, step):
        p, m = plus[1 - role], minus[1 - role]
        if step == 0:
            ref, target = lines(layer, role, own_at[role]), p
        elif step == 1:
            ref, target = lines(layer, role, own_at[role]), m
        elif step == 2:
            ref, target = half(lines(layer, role, minus_at[role]), 0), p
        else:
            ref, target = half(lines(layer, role, plus_at[role]), 1), m
        return remote(ref, ref, ss.at[layer, 4 + step], rs.at[layer, 5 + step], target)

    def s2_in(layer, role, step):
        if step == 0:
            ref = lines(layer, role, minus_at[role])
        elif step == 1:
            ref = lines(layer, role, plus_at[role])
        else:
            ref = half(lines(layer, role, far_at[role]), step - 2)
        return remote(ref, ref, ss.at[layer, 4 + step], rs.at[layer, 5 + step], plus[1 - role])

    def for_pair(p, guard, body):
        @pl.when(guard)
        def _():
            body(z - 2 * p, 0)

        @pl.when(jnp.logical_and(guard, z - 2 * p - 1 >= 0))
        def _():
            body(z - 2 * p - 1, 1)

    def ev0(p):
        def body(layer, role):
            @pl.when(layer < z)
            def _():
                zcopy(layer, me).wait_recv()

            s1(layer, role, 0).start()
            s1(layer, role, 1).start()

        for_pair(p, p < npairs, body)

    def ev1(p):
        def body(layer, role):
            s1_in(layer, role, 0).wait_recv()
            s1(layer, role, 2).start()
            s1_in(layer, role, 1).wait_recv()
            s1(layer, role, 3).start()

        for_pair(p, p < npairs, body)

    def ev2(p):
        def body(layer, role):
            s1_in(layer, role, 2).wait_recv()
            s1_in(layer, role, 3).wait_recv()
            s2(layer, role, 0).start()
            s2(layer, role, 1).start()

        for_pair(p, p < npairs, body)

    def ev3(p):
        def body(layer, role):
            s2_in(layer, role, 0).wait_recv()
            s2(layer, role, 2).start()
            s2_in(layer, role, 1).wait_recv()
            s2(layer, role, 3).start()

        for_pair(p, p < npairs, body)

    def ev4(p):
        def body(layer, role):
            s2_in(layer, role, 2).wait_recv()
            s2_in(layer, role, 3).wait_recv()

        for_pair(p, p < npairs, body)

    def acopy(step, target):
        return remote(anc, anc, ass.at[step], ars, target)

    in_first = x == 0
    a_root = jnp.logical_and(x == 0, y == 0)

    def anchor_in():
        acopy(0, me).wait_recv()

    @pl.loop(z + 1, NZ)
    def _(zz):
        zcopy(z, seq_of(zz, x, y)).start()

    ev0(0)

    @pl.when(me == 0)
    def _():
        for zz in range(1, NZ):
            acopy(zz - 1, seq_of(zz, 0, 0)).start()

    for j in range(8):
        for g in range(2):
            h = g * 8 + j
            qt[j // 4, g * HD : (g + 1) * HD, (j % 4) * TOK : (j % 4 + 1) * TOK] = q_ref[:, h * HD : (h + 1) * HD].T

    def simple_chunk(nb, causal):
        for r in range(NR):
            s = dot(kc[0, 0 : nb * 128], qt[r])
            if causal:
                key_tok = lax.broadcasted_iota(jnp.int32, (TOK, TOK), 0)
                query_tok = lax.broadcasted_iota(jnp.int32, (TOK, TOK), 1)
                bias = jnp.where(key_tok <= query_tok, 0.0, LOW)
                bias = jnp.concatenate([bias] * (R // TOK), axis=1)
                s = s + jnp.concatenate([bias] * 2, axis=0)
            sb[r, 0 : nb * 128] = s
            hb = nb * 64
            for g in range(2):
                old = mst[r, g : g + 1]
                new = jnp.maximum(old, jnp.max(s[g * hb : (g + 1) * hb], axis=0, keepdims=True))
                mst[r, g : g + 1] = new
                shrink[0, r, g : g + 1] = jnp.exp2((old - new) * CSC)
                pb[r, g * hb : (g + 1) * hb] = jnp.exp2((sb[r, g * hb : (g + 1) * hb] - new) * CSC).astype(BF16)
            accumulate(0, r, dot(vc[0, :, 0 : nb * 128], pb[r, 0 : nb * 128]))

    def accumulate(par, r, d):
        a0 = shrink[par, r, 0:1]
        a1 = shrink[par, r, 1:2]
        acc[r, 0:128] = acc[r, 0:128] * a0 + d[0:128]
        acc[r, 128:256] = acc[r, 128:256] * a1 + d[128:256]
        acc[r, 256:257] = acc[r, 256:257] * a0 + d[256:257]
        acc[r, 257:258] = acc[r, 257:258] * a1 + d[257:258]

    tag_row = lax.broadcasted_iota(jnp.int32, (16, 128), 0)

    def put_block(par, j, keys, vals, m0, m1):
        cols = slice(j * 128, (j + 1) * 128)
        zero = jnp.zeros((128, 128), BF16)
        kc[par, cols, 0:128] = jnp.where(m0 > 0, keys, zero)
        kc[par, cols, 128:256] = jnp.where(m1 > 0, keys, zero)
        vc[par, 0:128, cols] = jnp.where(m0 > 0, vals, zero)
        vc[par, 128:256, cols] = jnp.where(m1 > 0, vals, zero)
        ones = jnp.where(tag_row == 0, m0, jnp.where(tag_row == 1, m1, 0.0))
        vc[par, 256:272, cols] = ones.astype(BF16)

    one_row = jnp.ones((1, 128), F32)
    zero_row = jnp.zeros((1, 128), F32)

    acc[...] = jnp.zeros_like(acc)
    mst[...] = jnp.full_like(mst, LOW)
    for g in range(2):
        vt = v_ref[:, g * HD : (g + 1) * HD].T
        for i in range(2):
            put_block(
                0, 2 * g + i, k_ref[i * 128 : (i + 1) * 128, g * HD : (g + 1) * HD], vt[:, i * 128 : (i + 1) * 128],
                one_row if g == 0 else zero_row, one_row if g == 1 else zero_row,
            )
    simple_chunk(4, True)

    def blocks_of(chunk):
        out = []
        for layer, role, at in chunk:
            for i in range(4):
                bx, by = (at, i) if role == 0 else (i, at)
                ok = jnp.minimum(layer + 1, 1)
                out.append((ok * layer + (1 - ok) * z, ok * bx + (1 - ok) * x, ok * by + (1 - ok) * y))
        return out

    def masks(layer, bx, by):
        seen = jnp.where(layer * PLANE + bx * NY + by < me, 1.0, 0.0)
        t = kv[layer, bx, by, 256:272, :].astype(F32)[0:1]
        m1 = t * seen
        m0 = seen - m1
        return m0, m1

    def expand(chunk, par):
        for j, (layer, bx, by) in enumerate(blocks_of(chunk)):
            m0, m1 = masks(layer, bx, by)
            put_block(par, j, kv[layer, bx, by, 0:128, :], kv[layer, bx, by, 128:256, :], m0, m1)

    def score(chunk, par, r):
        s = dot(kc[par], qt[r])
        sb[r] = s
        m0o, m1o = mst[r, 0:1], mst[r, 1:2]
        m0, m1 = m0o, m1o
        ms = []
        for j, (layer, bx, by) in enumerate(blocks_of(chunk)):
            k0, k1 = masks(layer, bx, by)
            k0, k1 = widen(k0) > 0, widen(k1) > 0
            ms.append((k0, k1))
            top = jnp.max(s[j * 128 : (j + 1) * 128], axis=0, keepdims=True)
            m0 = jnp.maximum(m0, jnp.where(k0, top, LOW))
            m1 = jnp.maximum(m1, jnp.where(k1, top, LOW))
        mst[r, 0:1] = m0
        mst[r, 1:2] = m1
        for j, (k0, k1) in enumerate(ms):
            mb[r, j : j + 1] = jnp.where(k0, m0, jnp.where(k1, m1, HIGH))
        shrink[par, r, 0:1] = jnp.exp2((m0o - m0) * CSC)
        shrink[par, r, 1:2] = jnp.exp2((m1o - m1) * CSC)

    def weigh(r):
        for j in range(CB):
            rows = slice(j * 128, (j + 1) * 128)
            pb[r, rows] = jnp.exp2((sb[r, rows] - mb[r, j : j + 1]) * CSC).astype(BF16)

    def absorb(par, r):
        accumulate(par, r, dot(vc[par], pb[r]))

    def run_chunk(cur, nxt, par, between):
        score(cur, par, 1)
        absorb(1 - par, 1)
        weigh(0)
        between()
        expand(nxt, 1 - par)
        score(nxt, 1 - par, 0)
        absorb(par, 0)
        weigh(1)

    def chunk_a(p):
        return ((z - 2 * p, 0, x), (z - 2 * p - 1, 1, y))

    def chunk_b(p, k):
        la, lb = z - 2 * p, z - 2 * p - 1
        if k == 0:
            return ((la, 0, xm), (la, 0, xp))
        if k == 1:
            return ((lb, 1, ym), (lb, 1, yp))
        return ((la, 0, x2), (lb, 1, y2))

    def comm_a(i):
        ev0(i)
        ev1(i - 1)
        ev2(i - 2)

    ev0(1)
    ev1(0)
    ev0(2)
    ev1(1)
    ev2(0)

    @pl.when(a_root)
    def _():
        @pl.when(z > 0)
        def _():
            anchor_in()

        acopy(7, seq_of(z, 0, 1)).start()
        acopy(8, seq_of(z, 0, 3)).start()

    pb[1] = jnp.zeros_like(pb[1])
    vc[1] = jnp.zeros_like(vc[1])
    shrink[1] = jnp.ones_like(shrink[1])
    expand(chunk_a(0), 0)
    score(chunk_a(0), 0, 0)

    @pl.loop(0, npairs - 1)
    def _(p):
        run_chunk(chunk_a(p), chunk_a(p + 1), lax.rem(p, 2), functools.partial(comm_a, p + 3))

    run_chunk(chunk_a(npairs - 1), chunk_b(0, 0), lax.rem(npairs - 1, 2), functools.partial(ev3, 0))

    @pl.when(jnp.logical_and(in_first, y > 0))
    def _():
        anchor_in()

    @pl.when(jnp.logical_and(in_first, y == 1))
    def _():
        acopy(7, seq_of(z, 0, 2)).start()

    @pl.when(in_first)
    def _():
        acopy(9, seq_of(z, 1, y)).start()
        acopy(10, seq_of(z, 3, y)).start()

    @pl.loop(0, npairs)
    def _(p):
        par = lax.rem(npairs + 3 * p, 2)
        nxt = jnp.minimum(p + 1, npairs - 1)
        run_chunk(chunk_b(p, 0), chunk_b(p, 1), par, lambda: None)
        run_chunk(chunk_b(p, 1), chunk_b(p, 2), 1 - par, functools.partial(ev4, p))
        run_chunk(chunk_b(p, 2), chunk_b(nxt, 0), par, functools.partial(ev3, p + 1))

    absorb(1 - lax.rem(npairs * 4, 2), 1)

    @pl.when(x > 0)
    def _():
        anchor_in()

    @pl.when(x == 1)
    def _():
        acopy(9, seq_of(z, 2, y)).start()

    @pl.when(me > 0)
    def _():
        for g in range(2):
            put_block(
                0, g, anc[g, 0:128, :], anc[g, 128:256, :],
                one_row if g == 0 else zero_row, one_row if g == 1 else zero_row,
            )
        simple_chunk(2, False)

    for j in range(8):
        cols = slice((j % 4) * TOK, (j % 4 + 1) * TOK)
        for g in range(2):
            h = g * 8 + j
            total = acc[j // 4, 256 + g : 257 + g, cols]
            mixed = acc[j // 4, g * HD : (g + 1) * HD, cols] / total
            o_ref[:, h * HD : (h + 1) * HD] = mixed.astype(BF16).T

    @pl.loop(z + 1, NZ)
    def _(zz):
        zcopy(z, seq_of(zz, x, y)).wait_send()

    def drain(p):
        def body(layer, role):
            for step in range(4):
                s1(layer, role, step).wait_send()
                s2(layer, role, step).wait_send()

        for_pair(p, p < npairs, body)

    @pl.loop(0, npairs)
    def _(p):
        drain(p)

    @pl.when(me == 0)
    def _():
        for zz in range(1, NZ):
            acopy(zz - 1, me).wait_send()

    @pl.when(a_root)
    def _():
        acopy(7, me).wait_send()
        acopy(8, me).wait_send()

    @pl.when(jnp.logical_and(in_first, y == 1))
    def _():
        acopy(7, me).wait_send()

    @pl.when(in_first)
    def _():
        acopy(9, me).wait_send()
        acopy(10, me).wait_send()

    @pl.when(x == 1)
    def _():
        acopy(9, me).wait_send()


def per_device(queries, keys, values, kept_count, kept_rows):
    vmem = pl.BlockSpec(memory_space=pltpu.VMEM)
    return pl.pallas_call(
        kernel,
        out_shape=jax.ShapeDtypeStruct(queries.shape, BF16),
        in_specs=[vmem] * 5,
        out_specs=vmem,
        scratch_shapes=[
            pltpu.VMEM((NZ, NX, NY, BLK, 128), BF16),
            pltpu.VMEM((2, 256, 128), BF16),
            pltpu.VMEM((NR, 2 * HD, R), BF16),
            pltpu.VMEM((NR, BLK, R), F32),
            pltpu.VMEM((NR, 8, R), F32),
            pltpu.VMEM((2, NK, 2 * HD), BF16),
            pltpu.VMEM((2, BLK, NK), BF16),
            pltpu.VMEM((NR, NK, R), F32),
            pltpu.VMEM((NR, NK, R), BF16),
            pltpu.VMEM((NR, CB, R), F32),
            pltpu.VMEM((2, NR, 8, R), F32),
            pltpu.SemaphoreType.DMA((NZ, 9)),
            pltpu.SemaphoreType.DMA((NZ, 8)),
            pltpu.SemaphoreType.DMA((NZ,)),
            pltpu.SemaphoreType.DMA,
            pltpu.SemaphoreType.DMA((11,)),
        ],
        compiler_params=pltpu.CompilerParams(
            collective_id=0, has_side_effects=True, vmem_limit_bytes=56 * 2**20
        ),
        cost_estimate=pl.CostEstimate(flops=17_000_000_000, bytes_accessed=4_000_000, transcendentals=33_000_000),
    )(queries, keys, values, kept_count, kept_rows)


def solution(mesh):
    return jax.shard_map(
        per_device,
        mesh=mesh,
        in_specs=(
            P("seq", "head"),
            P("seq", "head"),
            P("seq", "head"),
            P("seq", "head"),
            P("seq", "head", None),
        ),
        out_specs=P("seq", "head"),
        check_vma=False,
    )
```

```python
import functools
import math

import jax
import jax.numpy as jnp
from jax import lax
from jax.experimental import pallas as pl
from jax.experimental.pallas import tpu as pltpu
from jax.sharding import PartitionSpec as P

F32 = jnp.float32
BF16 = jnp.bfloat16
HD = 128
TOK = 256
NZ, NX, NY = 8, 4, 4
PLANE = NX * NY
BLK = 272
CB = 8
NK = CB * 128
R = 1024
NR = 2
LOW = -1.0e30
HIGH = 1.0e30
CSC = math.log2(math.e) / math.sqrt(HD)


def dot(a, b):
    return jnp.dot(a, b, preferred_element_type=F32)


def dot_tn(a, b):
    return lax.dot_general(a, b, (((0,), (0,)), ((), ())), preferred_element_type=F32)


def widen(row):
    return jnp.concatenate([row] * (R // 128), axis=1)


def kernel(
    q_ref, k_ref, v_ref, cnt_ref, rows_ref, o_ref,
    kv, anc, qt, acc, mst, kc, vc, sb, pb, mb, shrink, msk,
    rs, ss, zs, ars, ass,
):
    me = lax.axis_index("seq")
    z = me // PLANE
    x = (me % PLANE) // NY
    y = me % NY
    npairs = z // 2 + 1

    def seq_of(zz, xx, yy):
        return zz * PLANE + xx * NY + yy

    xp, xm, x2 = (x + 1) % NX, (x + NX - 1) % NX, (x + 2) % NX
    yp, ym, y2 = (y + 1) % NY, (y + NY - 1) % NY, (y + 2) % NY
    plus = {0: seq_of(z, x, yp), 1: seq_of(z, xp, y)}
    minus = {0: seq_of(z, x, ym), 1: seq_of(z, xm, y)}
    far = {0: seq_of(z, x, y2), 1: seq_of(z, x2, y)}

    def remote(src, dst, send_sem, recv_sem, target):
        return pltpu.make_async_remote_copy(
            src_ref=src, dst_ref=dst, send_sem=send_sem, recv_sem=recv_sem,
            device_id={"seq": target}, device_id_type=pl.DeviceIdType.MESH,
        )

    barrier = pltpu.get_barrier_semaphore()
    for other in (plus[0], minus[0], far[0], plus[1], minus[1], far[1]):
        pl.semaphore_signal(barrier, inc=1, device_id={"seq": other}, device_id_type=pl.DeviceIdType.MESH)
    for dz in range(1, NZ):
        pl.semaphore_signal(
            barrier, inc=1, device_id={"seq": seq_of((z + dz) % NZ, x, y)}, device_id_type=pl.DeviceIdType.MESH
        )

    ksel = jnp.zeros((128, HD), F32)
    vsel = jnp.zeros((HD, 128), F32)
    tok_row = lax.broadcasted_iota(jnp.int32, (TOK, 128), 0)
    slot = lax.broadcasted_iota(jnp.int32, (1, 128), 1)
    for g in range(2):
        picks = jnp.where(slot < cnt_ref[0:1, g : g + 1], rows_ref[0, g : g + 1, :], -1)
        hot = jnp.where(tok_row == picks, 1.0, 0.0).astype(BF16)
        ksel = ksel + dot_tn(hot, k_ref[:, g * HD : (g + 1) * HD])
        vsel = vsel + dot_tn(v_ref[:, g * HD : (g + 1) * HD], hot)
    kv[z, x, y, 0:128, :] = ksel.astype(BF16)
    kv[z, x, y, 128:256, :] = vsel.astype(BF16)
    tag = jnp.where(cnt_ref[0:1, 1:2] > 0, 1.0, 0.0)
    kv[z, x, y, 256:272, :] = jnp.broadcast_to(tag, (16, 128)).astype(BF16)

    @pl.when(me == 0)
    def _():
        for g in range(2):
            anc[g, 0:128, :] = k_ref[0:128, g * HD : (g + 1) * HD]
            anc[g, 128:256, :] = v_ref[0:128, g * HD : (g + 1) * HD].T

    pl.semaphore_wait(barrier, 6 + NZ - 1)

    def lines(layer, role, at):
        return kv.at[layer, at] if role == 0 else kv.at[layer, :, at]

    def half(ref, which):
        return ref.at[:, 0:128] if which == 0 else ref.at[:, 128:BLK]

    own_at = {0: x, 1: y}
    minus_at = {0: xm, 1: ym}
    plus_at = {0: xp, 1: yp}
    far_at = {0: x2, 1: y2}

    def block(layer, role, at):
        return kv.at[layer, x, at] if role == 0 else kv.at[layer, at, y]

    b_own, b_minus, b_plus, b_far = {0: y, 1: x}, {0: ym, 1: xm}, {0: yp, 1: xp}, {0: y2, 1: x2}

    def zcopy(src_layer, target):
        ref = kv.at[src_layer, x, y]
        return remote(ref, ref, zs.at[target // PLANE], rs.at[src_layer, 0], target)

    def s1(layer, role, step):
        ref = block(layer, role, b_own[role])
        target = (plus, minus, far)[step][role]
        return remote(ref, ref, ss.at[layer, step], rs.at[layer, 1 + step], target)

    def s1_in(layer, role, step):
        ref = block(layer, role, (b_minus, b_plus, b_far)[step][role])
        return remote(ref, ref, ss.at[layer, step], rs.at[layer, 1 + step], plus[role])

    def s2(layer, role, step):
        p, m = plus[1 - role], minus[1 - role]
        if step < 2:
            ref, target = lines(layer, role, own_at[role]), (p, m)[step]
        elif step == 2:
            ref, target = half(lines(layer, role, minus_at[role]), 0), p
        else:
            ref, target = half(lines(layer, role, plus_at[role]), 1), m
        return remote(ref, ref, ss.at[layer, 3 + step], rs.at[layer, 4 + step], target)

    def s2_in(layer, role, step):
        if step < 2:
            ref = lines(layer, role, (minus_at, plus_at)[step][role])
        else:
            ref = half(lines(layer, role, far_at[role]), step - 2)
        return remote(ref, ref, ss.at[layer, 3 + step], rs.at[layer, 4 + step], plus[1 - role])

    def for_pair(p, guard, body):
        @pl.when(guard)
        def _():
            body(z - 2 * p, 0)

        @pl.when(jnp.logical_and(guard, z - 2 * p - 1 >= 0))
        def _():
            body(z - 2 * p - 1, 1)

    def ev0(p):
        def body(layer, role):
            @pl.when(layer < z)
            def _():
                zcopy(layer, me).wait_recv()
                for step in range(3):
                    s1(layer, role, step).start()

        for_pair(p, p < npairs, body)

    def ev1(p):
        def body(layer, role):
            for step in range(3):
                s1_in(layer, role, step).wait_recv()

        for_pair(p, p < npairs, body)

        @pl.when(p <= 0)
        def _():
            lines_out(p)

    def lines_out(p):
        def body(layer, role):
            s2(layer, role, 0).start()
            s2(layer, role, 1).start()

        for_pair(p, p < npairs, body)

    def ev3(p):
        def body(layer, role):
            s2_in(layer, role, 0).wait_recv()
            s2(layer, role, 2).start()
            s2_in(layer, role, 1).wait_recv()
            s2(layer, role, 3).start()

        for_pair(p, p < npairs, body)
        lines_out(p + 1)

    def ev4(p):
        def body(layer, role):
            s2_in(layer, role, 2).wait_recv()
            s2_in(layer, role, 3).wait_recv()

        for_pair(p, p < npairs, body)

    def acopy(step, target):
        return remote(anc, anc, ass.at[step], ars, target)

    in_first = x == 0
    a_root = jnp.logical_and(x == 0, y == 0)

    def anchor_in():
        acopy(0, me).wait_recv()

    for step in range(3):
        s1(z, 0, step).start()

    @pl.loop(z + 1, NZ)
    def _(zz):
        zcopy(z, seq_of(zz, x, y)).start()

    for j in range(8):
        for g in range(2):
            h = g * 8 + j
            qt[j // 4, g * HD : (g + 1) * HD, (j % 4) * TOK : (j % 4 + 1) * TOK] = q_ref[:, h * HD : (h + 1) * HD].T

    def simple_chunk(nb, causal):
        for r in range(NR):
            s = dot(kc[0, 0 : nb * 128], qt[r])
            if causal:
                key_tok = lax.broadcasted_iota(jnp.int32, (TOK, TOK), 0)
                query_tok = lax.broadcasted_iota(jnp.int32, (TOK, TOK), 1)
                bias = jnp.where(key_tok <= query_tok, 0.0, LOW)
                bias = jnp.concatenate([bias] * (R // TOK), axis=1)
                s = s + jnp.concatenate([bias] * 2, axis=0)
            sb[r, 0 : nb * 128] = s
            hb = nb * 64
            for g in range(2):
                old = mst[r, g : g + 1]
                new = jnp.maximum(old, jnp.max(s[g * hb : (g + 1) * hb], axis=0, keepdims=True))
                mst[r, g : g + 1] = new
                shrink[0, r, g : g + 1] = jnp.exp2((old - new) * CSC)
                pb[r, g * hb : (g + 1) * hb] = jnp.exp2((sb[r, g * hb : (g + 1) * hb] - new) * CSC).astype(BF16)
            accumulate(0, r, dot(vc[0, :, 0 : nb * 128], pb[r, 0 : nb * 128]))

    def accumulate(par, r, d):
        a0 = shrink[par, r, 0:1]
        a1 = shrink[par, r, 1:2]
        acc[r, 0:128] = acc[r, 0:128] * a0 + d[0:128]
        acc[r, 128:256] = acc[r, 128:256] * a1 + d[128:256]
        acc[r, 256:257] = acc[r, 256:257] * a0 + d[256:257]
        acc[r, 257:258] = acc[r, 257:258] * a1 + d[257:258]

    tag_row = lax.broadcasted_iota(jnp.int32, (16, 128), 0)

    def put_block(par, j, keys, vals, m0, m1):
        cols = slice(j * 128, (j + 1) * 128)
        zero = jnp.zeros((128, 128), BF16)
        kc[par, cols, 0:128] = jnp.where(m0 > 0, keys, zero)
        kc[par, cols, 128:256] = jnp.where(m1 > 0, keys, zero)
        vc[par, 0:128, cols] = jnp.where(m0 > 0, vals, zero)
        vc[par, 128:256, cols] = jnp.where(m1 > 0, vals, zero)
        ones = jnp.where(tag_row == 0, m0, jnp.where(tag_row == 1, m1, 0.0))
        vc[par, 256:272, cols] = ones.astype(BF16)

    one_row = jnp.ones((1, 128), F32)
    zero_row = jnp.zeros((1, 128), F32)

    acc[...] = jnp.zeros_like(acc)
    mst[...] = jnp.full_like(mst, LOW)
    for g in range(2):
        vt = v_ref[:, g * HD : (g + 1) * HD].T
        for i in range(2):
            put_block(
                0, 2 * g + i, k_ref[i * 128 : (i + 1) * 128, g * HD : (g + 1) * HD], vt[:, i * 128 : (i + 1) * 128],
                one_row if g == 0 else zero_row, one_row if g == 1 else zero_row,
            )
    simple_chunk(4, True)

    def blocks_of(chunk):
        out = []
        for layer, role, at in chunk:
            for i in range(4):
                bx, by = (at, i) if role == 0 else (i, at)
                ok = jnp.minimum(layer + 1, 1)
                out.append((ok * layer + (1 - ok) * z, ok * bx + (1 - ok) * x, ok * by + (1 - ok) * y))
        return out

    def masks(layer, bx, by):
        seen = jnp.where(layer * PLANE + bx * NY + by < me, 1.0, 0.0)
        t = kv[layer, bx, by, 256:272, :].astype(F32)[0:1]
        m1 = t * seen
        m0 = seen - m1
        return m0, m1

    def expand(chunk, par):
        for j, (layer, bx, by) in enumerate(blocks_of(chunk)):
            m0, m1 = masks(layer, bx, by)
            msk[par, j : j + 1] = m0
            msk[par, CB + j : CB + j + 1] = m1
            put_block(par, j, kv[layer, bx, by, 0:128, :], kv[layer, bx, by, 128:256, :], m0, m1)

    def score(par, r):
        s = dot(kc[par], qt[r])
        sb[r] = s
        m0o, m1o = mst[r, 0:1], mst[r, 1:2]
        m0, m1 = m0o, m1o
        ms = []
        for j in range(CB):
            k0, k1 = widen(msk[par, j : j + 1]) > 0, widen(msk[par, CB + j : CB + j + 1]) > 0
            ms.append((k0, k1))
            top = jnp.max(s[j * 128 : (j + 1) * 128], axis=0, keepdims=True)
            m0 = jnp.maximum(m0, jnp.where(k0, top, LOW))
            m1 = jnp.maximum(m1, jnp.where(k1, top, LOW))
        mst[r, 0:1] = m0
        mst[r, 1:2] = m1
        for j, (k0, k1) in enumerate(ms):
            mb[r, j : j + 1] = jnp.where(k0, m0, jnp.where(k1, m1, HIGH))
        shrink[par, r, 0:1] = jnp.exp2((m0o - m0) * CSC)
        shrink[par, r, 1:2] = jnp.exp2((m1o - m1) * CSC)

    def weigh(r):
        for j in range(CB):
            rows = slice(j * 128, (j + 1) * 128)
            pb[r, rows] = jnp.exp2((sb[r, rows] - mb[r, j : j + 1]) * CSC).astype(BF16)

    def absorb(par, r):
        accumulate(par, r, dot(vc[par], pb[r]))

    def run_chunk(nxt, par, between):
        score(par, 1)
        absorb(1 - par, 1)
        weigh(0)
        between()
        expand(nxt, 1 - par)
        score(1 - par, 0)
        absorb(par, 0)
        weigh(1)

    def chunk_a(p):
        return ((z - 2 * p, 0, x), (z - 2 * p - 1, 1, y))

    def chunk_b(p, k):
        la, lb = z - 2 * p, z - 2 * p - 1
        if k == 0:
            return ((la, 0, xm), (la, 0, xp))
        if k == 1:
            return ((lb, 1, ym), (lb, 1, yp))
        return ((la, 0, x2), (lb, 1, y2))

    def comm_a(i):
        ev0(i)
        ev1(i - 1)

    ev0(0)
    ev1(0)
    ev0(1)

    @pl.when(me == 0)
    def _():
        for zz in range(1, NZ):
            acopy(zz - 1, seq_of(zz, 0, 0)).start()

    def anchor_along_y():
        @pl.when(a_root)
        def _():
            @pl.when(z > 0)
            def _():
                anchor_in()

            for i in range(3):
                acopy(7 + i, seq_of(z, 0, i + 1)).start()

    def anchor_along_x():
        @pl.when(in_first)
        def _():
            @pl.when(y > 0)
            def _():
                anchor_in()

            for i in range(3):
                acopy(10 + i, seq_of(z, i + 1, y)).start()

    pb[1] = jnp.zeros_like(pb[1])
    vc[1] = jnp.zeros_like(vc[1])
    shrink[1] = jnp.ones_like(shrink[1])
    expand(chunk_a(0), 0)
    score(0, 0)

    @pl.loop(0, npairs - 1)
    def _(p):
        run_chunk(chunk_a(p + 1), lax.rem(p, 2), functools.partial(comm_a, p + 2))

    run_chunk(chunk_b(0, 0), lax.rem(npairs - 1, 2), functools.partial(ev3, 0))

    @pl.loop(0, npairs)
    def _(p):
        par = lax.rem(npairs + 3 * p, 2)

        def near():
            @pl.when(p == 0)
            def _():
                anchor_along_y()

        def away():
            ev4(p)

            @pl.when(p == jnp.minimum(1, npairs - 1))
            def _():
                anchor_along_x()

        run_chunk(chunk_b(p, 1), par, near)
        run_chunk(chunk_b(p, 2), 1 - par, away)
        run_chunk(chunk_b(jnp.minimum(p + 1, npairs - 1), 0), par, functools.partial(ev3, p + 1))

    absorb(1 - lax.rem(npairs * 4, 2), 1)

    @pl.when(x > 0)
    def _():
        anchor_in()

    @pl.when(me > 0)
    def _():
        for g in range(2):
            put_block(
                0, g, anc[g, 0:128, :], anc[g, 128:256, :],
                one_row if g == 0 else zero_row, one_row if g == 1 else zero_row,
            )
        simple_chunk(2, False)

    for j in range(8):
        cols = slice((j % 4) * TOK, (j % 4 + 1) * TOK)
        for g in range(2):
            h = g * 8 + j
            total = acc[j // 4, 256 + g : 257 + g, cols]
            mixed = acc[j // 4, g * HD : (g + 1) * HD, cols] / total
            o_ref[:, h * HD : (h + 1) * HD] = mixed.astype(BF16).T

    @pl.loop(z + 1, NZ)
    def _(zz):
        zcopy(z, seq_of(zz, x, y)).wait_send()

    def drain(p):
        def body(layer, role):
            for step in range(3):
                s1(layer, role, step).wait_send()
            for step in range(4):
                s2(layer, role, step).wait_send()

        for_pair(p, p < npairs, body)

    @pl.loop(0, npairs)
    def _(p):
        drain(p)

    @pl.when(me == 0)
    def _():
        for zz in range(1, NZ):
            acopy(zz - 1, me).wait_send()

    @pl.when(a_root)
    def _():
        for i in range(3):
            acopy(7 + i, me).wait_send()

    @pl.when(in_first)
    def _():
        for i in range(3):
            acopy(10 + i, me).wait_send()


def per_device(queries, keys, values, kept_count, kept_rows):
    vmem = pl.BlockSpec(memory_space=pltpu.VMEM)
    return pl.pallas_call(
        kernel,
        out_shape=jax.ShapeDtypeStruct(queries.shape, BF16),
        in_specs=[vmem] * 5,
        out_specs=vmem,
        scratch_shapes=[
            pltpu.VMEM((NZ, NX, NY, BLK, 128), BF16),
            pltpu.VMEM((2, 256, 128), BF16),
            pltpu.VMEM((NR, 2 * HD, R), BF16),
            pltpu.VMEM((NR, BLK, R), F32),
            pltpu.VMEM((NR, 8, R), F32),
            pltpu.VMEM((2, NK, 2 * HD), BF16),
            pltpu.VMEM((2, BLK, NK), BF16),
            pltpu.VMEM((NR, NK, R), F32),
            pltpu.VMEM((NR, NK, R), BF16),
            pltpu.VMEM((NR, CB, R), F32),
            pltpu.VMEM((2, NR, 8, R), F32),
            pltpu.VMEM((2, 2 * CB, 128), F32),
            pltpu.SemaphoreType.DMA((NZ, 8)),
            pltpu.SemaphoreType.DMA((NZ, 8)),
            pltpu.SemaphoreType.DMA((NZ,)),
            pltpu.SemaphoreType.DMA,
            pltpu.SemaphoreType.DMA((13,)),
        ],
        compiler_params=pltpu.CompilerParams(
            collective_id=0, has_side_effects=True, vmem_limit_bytes=56 * 2**20
        ),
        cost_estimate=pl.CostEstimate(flops=17_000_000_000, bytes_accessed=4_000_000, transcendentals=33_000_000),
    )(queries, keys, values, kept_count, kept_rows)


def solution(mesh):
    return jax.shard_map(
        per_device,
        mesh=mesh,
        in_specs=(
            P("seq", "head"),
            P("seq", "head"),
            P("seq", "head"),
            P("seq", "head"),
            P("seq", "head", None),
        ),
        out_specs=P("seq", "head"),
        check_vma=False,
    )
```

```python
import functools
import math

import jax
import jax.numpy as jnp
from jax import lax
from jax.experimental import pallas as pl
from jax.experimental.pallas import tpu as pltpu
from jax.sharding import PartitionSpec as P

F32 = jnp.float32
BF16 = jnp.bfloat16
HD = 128
TOK = 256
NZ, NX, NY = 8, 4, 4
PLANE = NX * NY
BLK = 272
CB = 8
NK = CB * 128
R = 1024
NR = 2
LOW = -1.0e30
HIGH = 1.0e30
CSC = math.log2(math.e) / math.sqrt(HD)


def dot(a, b):
    return jnp.dot(a, b, preferred_element_type=F32)


def dot_tn(a, b):
    return lax.dot_general(a, b, (((0,), (0,)), ((), ())), preferred_element_type=F32)


def widen(row):
    return jnp.concatenate([row] * (R // 128), axis=1)


def kernel(
    q_ref, k_ref, v_ref, cnt_ref, rows_ref, o_ref,
    kv, anc, qt, acc, mst, kc, vc, sb, pb, mb, shrink, msk, tot,
    rs, ss, zs, ars, ass,
):
    me = lax.axis_index("seq")
    z = me // PLANE
    x = (me % PLANE) // NY
    y = me % NY
    npairs = z // 2 + 1

    def seq_of(zz, xx, yy):
        return zz * PLANE + xx * NY + yy

    xp, xm, x2 = (x + 1) % NX, (x + NX - 1) % NX, (x + 2) % NX
    yp, ym, y2 = (y + 1) % NY, (y + NY - 1) % NY, (y + 2) % NY
    plus = {0: seq_of(z, x, yp), 1: seq_of(z, xp, y)}
    minus = {0: seq_of(z, x, ym), 1: seq_of(z, xm, y)}
    far = {0: seq_of(z, x, y2), 1: seq_of(z, x2, y)}

    def remote(src, dst, send_sem, recv_sem, target):
        return pltpu.make_async_remote_copy(
            src_ref=src, dst_ref=dst, send_sem=send_sem, recv_sem=recv_sem,
            device_id={"seq": target}, device_id_type=pl.DeviceIdType.MESH,
        )

    barrier = pltpu.get_barrier_semaphore()
    for other in (plus[0], minus[0], far[0], plus[1], minus[1], far[1]):
        pl.semaphore_signal(barrier, inc=1, device_id={"seq": other}, device_id_type=pl.DeviceIdType.MESH)
    for dz in range(1, NZ):
        pl.semaphore_signal(
            barrier, inc=1, device_id={"seq": seq_of((z + dz) % NZ, x, y)}, device_id_type=pl.DeviceIdType.MESH
        )

    ksel = jnp.zeros((128, HD), F32)
    vsel = jnp.zeros((HD, 128), F32)
    tok_row = lax.broadcasted_iota(jnp.int32, (TOK, 128), 0)
    slot = lax.broadcasted_iota(jnp.int32, (1, 128), 1)
    for g in range(2):
        picks = jnp.where(slot < cnt_ref[0:1, g : g + 1], rows_ref[0, g : g + 1, :], -1)
        hot = jnp.where(tok_row == picks, 1.0, 0.0).astype(BF16)
        ksel = ksel + dot_tn(hot, k_ref[:, g * HD : (g + 1) * HD])
        vsel = vsel + dot_tn(v_ref[:, g * HD : (g + 1) * HD], hot)
    kv[z, x, y, 0:128, :] = ksel.astype(BF16)
    kv[z, x, y, 128:256, :] = vsel.astype(BF16)
    tag = jnp.where(cnt_ref[0:1, 1:2] > 0, 1.0, 0.0)
    kv[z, x, y, 256:272, :] = jnp.broadcast_to(tag, (16, 128)).astype(BF16)

    @pl.when(me == 0)
    def _():
        for g in range(2):
            anc[g, 0:128, :] = k_ref[0:128, g * HD : (g + 1) * HD]
            anc[g, 128:256, :] = v_ref[0:128, g * HD : (g + 1) * HD].T

    pl.semaphore_wait(barrier, 6 + NZ - 1)

    def lines(layer, role, at):
        return kv.at[layer, at] if role == 0 else kv.at[layer, :, at]

    def half(ref, which):
        return ref.at[:, 0:128] if which == 0 else ref.at[:, 128:BLK]

    own_at = {0: x, 1: y}
    minus_at = {0: xm, 1: ym}
    plus_at = {0: xp, 1: yp}
    far_at = {0: x2, 1: y2}

    def block(layer, role, at):
        return kv.at[layer, x, at] if role == 0 else kv.at[layer, at, y]

    b_own, b_minus, b_plus, b_far = {0: y, 1: x}, {0: ym, 1: xm}, {0: yp, 1: xp}, {0: y2, 1: x2}

    def zcopy(src_layer, target):
        ref = kv.at[src_layer, x, y]
        return remote(ref, ref, zs.at[target // PLANE], rs.at[src_layer, 0], target)

    def s1(layer, role, step):
        ref = block(layer, role, b_own[role])
        target = (plus, minus, far)[step][role]
        return remote(ref, ref, ss.at[layer, step], rs.at[layer, 1 + step], target)

    def s1_in(layer, role, step):
        ref = block(layer, role, (b_minus, b_plus, b_far)[step][role])
        return remote(ref, ref, ss.at[layer, step], rs.at[layer, 1 + step], plus[role])

    def s2(layer, role, step):
        p, m = plus[1 - role], minus[1 - role]
        if step < 2:
            ref, target = lines(layer, role, own_at[role]), (p, m)[step]
        elif step == 2:
            ref, target = half(lines(layer, role, minus_at[role]), 0), p
        else:
            ref, target = half(lines(layer, role, plus_at[role]), 1), m
        return remote(ref, ref, ss.at[layer, 3 + step], rs.at[layer, 4 + step], target)

    def s2_in(layer, role, step):
        if step < 2:
            ref = lines(layer, role, (minus_at, plus_at)[step][role])
        else:
            ref = half(lines(layer, role, far_at[role]), step - 2)
        return remote(ref, ref, ss.at[layer, 3 + step], rs.at[layer, 4 + step], plus[1 - role])

    def for_pair(p, guard, body):
        @pl.when(guard)
        def _():
            body(z - 2 * p, 0)

        @pl.when(jnp.logical_and(guard, z - 2 * p - 1 >= 0))
        def _():
            body(z - 2 * p - 1, 1)

    def ev0(p):
        def body(layer, role):
            @pl.when(layer < z)
            def _():
                zcopy(layer, me).wait_recv()
                for step in range(3):
                    s1(layer, role, step).start()

        for_pair(p, p < npairs, body)

    def ev1(p):
        def body(layer, role):
            for step in range(3):
                s1_in(layer, role, step).wait_recv()

        for_pair(p, p < npairs, body)

        @pl.when(p <= 0)
        def _():
            lines_out(p)

    def lines_out(p):
        def body(layer, role):
            s2(layer, role, 0).start()
            s2(layer, role, 1).start()

        for_pair(p, p < npairs, body)

    def ev3(p):
        def body(layer, role):
            s2_in(layer, role, 0).wait_recv()
            s2(layer, role, 2).start()
            s2_in(layer, role, 1).wait_recv()
            s2(layer, role, 3).start()

        for_pair(p, p < npairs, body)
        lines_out(p + 1)

    def ev4(p):
        def body(layer, role):
            s2_in(layer, role, 2).wait_recv()
            s2_in(layer, role, 3).wait_recv()

        for_pair(p, p < npairs, body)

    def acopy(step, target):
        return remote(anc, anc, ass.at[step], ars, target)

    in_first = x == 0
    a_root = jnp.logical_and(x == 0, y == 0)

    def anchor_in():
        acopy(0, me).wait_recv()

    for step in range(3):
        s1(z, 0, step).start()

    @pl.loop(z + 1, NZ)
    def _(zz):
        zcopy(z, seq_of(zz, x, y)).start()

    for j in range(8):
        for g in range(2):
            h = g * 8 + j
            qt[j // 4, g * HD : (g + 1) * HD, (j % 4) * TOK : (j % 4 + 1) * TOK] = q_ref[:, h * HD : (h + 1) * HD].T

    def simple_chunk(nb, causal):
        for r in range(NR):
            s = dot(kc[0, 0 : nb * 128], qt[r])
            if causal:
                key_tok = lax.broadcasted_iota(jnp.int32, (TOK, TOK), 0)
                query_tok = lax.broadcasted_iota(jnp.int32, (TOK, TOK), 1)
                bias = jnp.where(key_tok <= query_tok, 0.0, LOW)
                bias = jnp.concatenate([bias] * (R // TOK), axis=1)
                s = s + jnp.concatenate([bias] * 2, axis=0)
            sb[r, 0 : nb * 128] = s
            hb = nb * 64
            for g in range(2):
                old = mst[r, g : g + 1]
                new = jnp.maximum(old, jnp.max(s[g * hb : (g + 1) * hb], axis=0, keepdims=True))
                mst[r, g : g + 1] = new
                shrink[0, r, g : g + 1] = jnp.exp2((old - new) * CSC)
                w = jnp.exp2((sb[r, g * hb : (g + 1) * hb] - new) * CSC)
                pb[r, g * hb : (g + 1) * hb] = w.astype(BF16)
                tot[r, g : g + 1] = tot[r, g : g + 1] * shrink[0, r, g : g + 1] + jnp.sum(w, axis=0, keepdims=True)
            accumulate(0, r, dot(vc[0, :, 0 : nb * 128], pb[r, 0 : nb * 128]))

    def accumulate(par, r, d):
        a0 = shrink[par, r, 0:1]
        a1 = shrink[par, r, 1:2]
        acc[r, 0:128] = acc[r, 0:128] * a0 + d[0:128]
        acc[r, 128:256] = acc[r, 128:256] * a1 + d[128:256]

    def put_block(par, j, keys, vals, m0, m1):
        cols = slice(j * 128, (j + 1) * 128)
        zero = jnp.zeros((128, 128), BF16)
        kc[par, cols, 0:128] = jnp.where(m0 > 0, keys, zero)
        kc[par, cols, 128:256] = jnp.where(m1 > 0, keys, zero)
        vc[par, 0:128, cols] = jnp.where(m0 > 0, vals, zero)
        vc[par, 128:256, cols] = jnp.where(m1 > 0, vals, zero)

    one_row = jnp.ones((1, 128), F32)
    zero_row = jnp.zeros((1, 128), F32)

    acc[...] = jnp.zeros_like(acc)
    tot[...] = jnp.zeros_like(tot)
    mst[...] = jnp.full_like(mst, LOW)
    for g in range(2):
        vt = v_ref[:, g * HD : (g + 1) * HD].T
        for i in range(2):
            put_block(
                0, 2 * g + i, k_ref[i * 128 : (i + 1) * 128, g * HD : (g + 1) * HD], vt[:, i * 128 : (i + 1) * 128],
                one_row if g == 0 else zero_row, one_row if g == 1 else zero_row,
            )
    simple_chunk(4, True)

    def blocks_of(chunk):
        out = []
        for layer, role, at in chunk:
            for i in range(4):
                bx, by = (at, i) if role == 0 else (i, at)
                ok = jnp.minimum(layer + 1, 1)
                out.append((ok * layer + (1 - ok) * z, ok * bx + (1 - ok) * x, ok * by + (1 - ok) * y))
        return out

    def masks(layer, bx, by):
        seen = jnp.where(layer * PLANE + bx * NY + by < me, 1.0, 0.0)
        t = kv[layer, bx, by, 256:272, :].astype(F32)[0:1]
        m1 = t * seen
        m0 = seen - m1
        return m0, m1

    def expand(chunk, par):
        for j, (layer, bx, by) in enumerate(blocks_of(chunk)):
            m0, m1 = masks(layer, bx, by)
            msk[par, j : j + 1] = m0
            msk[par, CB + j : CB + j + 1] = m1
            put_block(par, j, kv[layer, bx, by, 0:128, :], kv[layer, bx, by, 128:256, :], m0, m1)

    def score(par, r):
        s = dot(kc[par], qt[r])
        sb[r] = s
        m0o, m1o = mst[r, 0:1], mst[r, 1:2]
        m0, m1 = m0o, m1o
        ms = []
        for j in range(CB):
            k0, k1 = widen(msk[par, j : j + 1]) > 0, widen(msk[par, CB + j : CB + j + 1]) > 0
            ms.append((k0, k1))
            top = jnp.max(s[j * 128 : (j + 1) * 128], axis=0, keepdims=True)
            m0 = jnp.maximum(m0, jnp.where(k0, top, LOW))
            m1 = jnp.maximum(m1, jnp.where(k1, top, LOW))
        mst[r, 0:1] = m0
        mst[r, 1:2] = m1
        for j, (k0, k1) in enumerate(ms):
            mb[r, j : j + 1] = jnp.where(k0, m0, jnp.where(k1, m1, HIGH))
        shrink[par, r, 0:1] = jnp.exp2((m0o - m0) * CSC)
        shrink[par, r, 1:2] = jnp.exp2((m1o - m1) * CSC)

    def weigh(par, r):
        t0 = tot[r, 0:1] * shrink[par, r, 0:1]
        t1 = tot[r, 1:2] * shrink[par, r, 1:2]
        for j in range(CB):
            rows = slice(j * 128, (j + 1) * 128)
            w = jnp.exp2((sb[r, rows] - mb[r, j : j + 1]) * CSC)
            pb[r, rows] = w.astype(BF16)
            part = jnp.sum(w, axis=0, keepdims=True)
            t0 = t0 + part * widen(msk[par, j : j + 1])
            t1 = t1 + part * widen(msk[par, CB + j : CB + j + 1])
        tot[r, 0:1] = t0
        tot[r, 1:2] = t1

    def absorb(par, r):
        accumulate(par, r, dot(vc[par], pb[r]))

    def run_chunk(nxt, par, between):
        score(par, 1)
        absorb(1 - par, 1)
        weigh(par, 0)
        between()
        expand(nxt, 1 - par)
        score(1 - par, 0)
        absorb(par, 0)
        weigh(par, 1)

    def chunk_a(p):
        return ((z - 2 * p, 0, x), (z - 2 * p - 1, 1, y))

    def chunk_b(p, k):
        la, lb = z - 2 * p, z - 2 * p - 1
        if k == 0:
            return ((la, 0, xm), (la, 0, xp))
        if k == 1:
            return ((lb, 1, ym), (lb, 1, yp))
        return ((la, 0, x2), (lb, 1, y2))

    def comm_a(i):
        ev0(i)
        ev1(i - 1)

    ev0(0)
    ev1(0)
    ev0(1)

    @pl.when(me == 0)
    def _():
        for zz in range(1, NZ):
            acopy(zz - 1, seq_of(zz, 0, 0)).start()

    def anchor_along_y():
        @pl.when(a_root)
        def _():
            @pl.when(z > 0)
            def _():
                anchor_in()

            for i in range(3):
                acopy(7 + i, seq_of(z, 0, i + 1)).start()

    def anchor_along_x():
        @pl.when(in_first)
        def _():
            @pl.when(y > 0)
            def _():
                anchor_in()

            for i in range(3):
                acopy(10 + i, seq_of(z, i + 1, y)).start()

    pb[1] = jnp.zeros_like(pb[1])
    vc[1] = jnp.zeros_like(vc[1])
    shrink[1] = jnp.ones_like(shrink[1])
    expand(chunk_a(0), 0)
    score(0, 0)

    @pl.loop(0, npairs - 1)
    def _(p):
        run_chunk(chunk_a(p + 1), lax.rem(p, 2), functools.partial(comm_a, p + 2))

    run_chunk(chunk_b(0, 0), lax.rem(npairs - 1, 2), functools.partial(ev3, 0))

    @pl.loop(0, npairs)
    def _(p):
        par = lax.rem(npairs + 3 * p, 2)

        def near():
            @pl.when(p == 0)
            def _():
                anchor_along_y()

        def away():
            ev4(p)

            @pl.when(p == jnp.minimum(1, npairs - 1))
            def _():
                anchor_along_x()

        run_chunk(chunk_b(p, 1), par, near)
        run_chunk(chunk_b(p, 2), 1 - par, away)
        run_chunk(chunk_b(jnp.minimum(p + 1, npairs - 1), 0), par, functools.partial(ev3, p + 1))

    absorb(1 - lax.rem(npairs * 4, 2), 1)

    @pl.when(x > 0)
    def _():
        anchor_in()

    @pl.when(me > 0)
    def _():
        for g in range(2):
            put_block(
                0, g, anc[g, 0:128, :], anc[g, 128:256, :],
                one_row if g == 0 else zero_row, one_row if g == 1 else zero_row,
            )
        simple_chunk(2, False)

    for j in range(8):
        cols = slice((j % 4) * TOK, (j % 4 + 1) * TOK)
        for g in range(2):
            h = g * 8 + j
            total = tot[j // 4, g : g + 1, cols]
            mixed = acc[j // 4, g * HD : (g + 1) * HD, cols] / total
            o_ref[:, h * HD : (h + 1) * HD] = mixed.astype(BF16).T

    @pl.loop(z + 1, NZ)
    def _(zz):
        zcopy(z, seq_of(zz, x, y)).wait_send()

    def drain(p):
        def body(layer, role):
            for step in range(3):
                s1(layer, role, step).wait_send()
            for step in range(4):
                s2(layer, role, step).wait_send()

        for_pair(p, p < npairs, body)

    @pl.loop(0, npairs)
    def _(p):
        drain(p)

    @pl.when(me == 0)
    def _():
        for zz in range(1, NZ):
            acopy(zz - 1, me).wait_send()

    @pl.when(a_root)
    def _():
        for i in range(3):
            acopy(7 + i, me).wait_send()

    @pl.when(in_first)
    def _():
        for i in range(3):
            acopy(10 + i, me).wait_send()


def per_device(queries, keys, values, kept_count, kept_rows):
    vmem = pl.BlockSpec(memory_space=pltpu.VMEM)
    return pl.pallas_call(
        kernel,
        out_shape=jax.ShapeDtypeStruct(queries.shape, BF16),
        in_specs=[vmem] * 5,
        out_specs=vmem,
        scratch_shapes=[
            pltpu.VMEM((NZ, NX, NY, BLK, 128), BF16),
            pltpu.VMEM((2, 256, 128), BF16),
            pltpu.VMEM((NR, 2 * HD, R), BF16),
            pltpu.VMEM((NR, 2 * HD, R), F32),
            pltpu.VMEM((NR, 8, R), F32),
            pltpu.VMEM((2, NK, 2 * HD), BF16),
            pltpu.VMEM((2, 2 * HD, NK), BF16),
            pltpu.VMEM((NR, NK, R), F32),
            pltpu.VMEM((NR, NK, R), BF16),
            pltpu.VMEM((NR, CB, R), F32),
            pltpu.VMEM((2, NR, 8, R), F32),
            pltpu.VMEM((2, 2 * CB, 128), F32),
            pltpu.VMEM((NR, 8, R), F32),
            pltpu.SemaphoreType.DMA((NZ, 8)),
            pltpu.SemaphoreType.DMA((NZ, 8)),
            pltpu.SemaphoreType.DMA((NZ,)),
            pltpu.SemaphoreType.DMA,
            pltpu.SemaphoreType.DMA((13,)),
        ],
        compiler_params=pltpu.CompilerParams(
            collective_id=0, has_side_effects=True, vmem_limit_bytes=56 * 2**20
        ),
        cost_estimate=pl.CostEstimate(flops=17_000_000_000, bytes_accessed=4_000_000, transcendentals=33_000_000),
    )(queries, keys, values, kept_count, kept_rows)


def solution(mesh):
    return jax.shard_map(
        per_device,
        mesh=mesh,
        in_specs=(
            P("seq", "head"),
            P("seq", "head"),
            P("seq", "head"),
            P("seq", "head"),
            P("seq", "head", None),
        ),
        out_specs=P("seq", "head"),
        check_vma=False,
    )
```
